256 devices in a mesh: gz: 4 (over z_hi), gy: 8 (over x, core), gx: 8 (over z_lo, y).
Axes of the slice: x: 4, y: 4, z: 8 (z_hi: 4, z_lo: 2; z = z_hi * 2 + z_lo), core: 2. Of those that a mesh axis runs over, the one named last changes fastest.
Arguments:
- cotangent: bfloat16 [4, 128, 128, 384], P('gz', 'gy', 'gx'), may hold values from -6 to 6
- saved_codes: bfloat16 [3, 4, 128, 128, 384], P(None, 'gz', 'gy', 'gx'), may hold values from -448 to 448
- saved_scales: bfloat16 [3, 4, 128, 128, 3], P(None, 'gz', 'gy', 'gx'), may hold values from 0.0039978027 to 0.049804688
- gains: float32 [3, 384], replicated, may hold values from 0.1 to 1.9
- w_qkv: bfloat16 [3, 384, 1152], replicated, may hold values from -1 to 1
- w_out: bfloat16 [3, 384, 384], replicated, may hold values from -0.3125 to 0.3125
Outputs:
- grad_input: bfloat16 [4, 128, 128, 384], P('gz', 'gy', 'gx')
- weight_grads: float32 [1536, 1152], P(('gz', 'gy', 'gx'))
The draws below stay inside these ranges and needn't reach their ends.
All inputs are finite; a program needn't handle non-finite values.
Results may differ from the reference program's by a relative error of at most 0.015.
Values may be sent and summed in bfloat16 or wider, within the bound.
No kernel may reach another device: no remote copies, remote signals or barrier semaphores. Data moves between devices by JAX's collectives and lax.ppermute only.
A program may use at most 128 MiB of HBM per device.

```python
import math
import jax
import jax.numpy as jnp
from jax import lax

C = 384
HEADS = 6
HEAD = 64
LAYERS = 3
BLK = 3
Z = 4
Y = 128
X = 128
TOKENS = 65536


def draw_w_qkv(key, part):
    key = jax.random.fold_in(key, 11)
    first_key = jax.random.fold_in(key, 0)
    normal_draw = jnp.clip(jax.random.normal(first_key, (LAYERS, C, 3 * C), jnp.float32), -6.0, 6.0)
    return (normal_draw / math.sqrt(C)).astype(jnp.bfloat16)


def level_of(own_key, extent, shards, smallest, high):
    def one(dim, blocks):
        steps = jax.random.uniform(jax.random.fold_in(jax.random.fold_in(own_key, 6), dim), (blocks,), jnp.float32, smallest / len(shards), high / len(shards))
        return jnp.repeat(jnp.exp(steps), extent[dim] // blocks).reshape((-1,) + (1,) * (len(extent) - dim - 1))

    factor_of = one(*shards[0])
    for cut in shards[1:]:
        factor_of = factor_of * one(*cut)
    return factor_of


def noise(rng, extent, deviation, reach, cuts=(), held_as=jnp.bfloat16):
    array = jax.random.normal(rng, extent, jnp.float32) * deviation
    if len(cuts) > 0:
        array = level_of(rng, extent, cuts, -0.22, 0.18) * array
    return jnp.clip(array, min=-reach, max=reach).astype(held_as)


def setup_inputs(seed: int = 0) -> dict:
    splits = jax.random.split(jax.random.key(seed), 7)
    cotangent = noise(splits[0], (Z, Y, X, C), 1.0, 6.0, ((0, 4), (1, 8), (2, 8)))
    saved_codes = noise(splits[1], (LAYERS, Z, Y, X, C), 64.0, 448.0, ((1, 4), (2, 8), (3, 8)))
    saved_scales = jnp.clip(jnp.exp(math.log(0.049804688) - 2.5223642 * jax.random.uniform(splits[2], (LAYERS, Z, Y, X, BLK), jnp.float32) ** level_of(splits[2], (LAYERS, Z, Y, X, BLK), ((1, 4), (2, 8), (3, 8)), -0.2, 0.2)), 0.0039978027, 0.049804688).astype(jnp.bfloat16)
    gains = jnp.clip(1.0 + 0.18 * jax.random.normal(splits[3], (LAYERS, C), jnp.float32), 0.1, 1.9)
    w_qkv = draw_w_qkv(jax.random.fold_in(splits[6], 71), 0)
    w_out = noise(splits[5], (LAYERS, C, C), C ** -0.5, 0.3125)
    return dict(cotangent=cotangent, saved_codes=saved_codes, saved_scales=saved_scales, gains=gains, w_qkv=w_qkv, w_out=w_out)


def widen(quant_codes, quant_scales):
    full_shape = quant_codes.shape
    blocks = quant_scales.shape[-1]
    grouped = quant_codes.astype(jnp.float32).reshape(full_shape[:-1] + (blocks, full_shape[-1] // blocks))
    return (grouped * quant_scales.astype(jnp.float32)[..., None]).reshape(full_shape)

def layer_back(hidden, stream, gain_row, w_qkv, w_out):
    outer_n, length, inner_n, width = hidden.shape
    mean_val = lax.optimization_barrier(jnp.mean(hidden, axis=-1, keepdims=True))
    centred = hidden - mean_val
    rstd_val = lax.rsqrt(lax.optimization_barrier(jnp.mean(centred * centred, axis=-1, keepdims=True)) + 1e-05)
    normal_form = centred * rstd_val
    normed = (normal_form * gain_row).astype(jnp.bfloat16)
    flat_normed = normed.reshape(-1, width)
    packed = jnp.dot(flat_normed, w_qkv, preferred_element_type=jnp.float32).astype(jnp.bfloat16)
    packed = packed.reshape(outer_n, length, inner_n, 3, HEADS, HEAD).astype(jnp.float32)
    queries = packed[:, :, :, 0]
    keys_all = packed[:, :, :, 1]
    values = packed[:, :, :, 2]
    factor = 1.0 / math.sqrt(HEAD)
    scores = jnp.einsum('aqbhd,akbhd->abhqk', queries, keys_all) * factor
    row_top = lax.optimization_barrier(jnp.max(scores, axis=-1, keepdims=True))
    exp_scores = jnp.exp(scores - row_top)
    attn_probs = exp_scores / lax.optimization_barrier(jnp.sum(exp_scores, axis=-1, keepdims=True))
    probs_low = attn_probs.astype(jnp.bfloat16).astype(jnp.float32)
    attended = jnp.einsum('abhqk,akbhd->aqbhd', probs_low, values).astype(jnp.bfloat16)
    grad_flat = stream.reshape(-1, width)
    grad_attended = jnp.dot(grad_flat, w_out.T, preferred_element_type=jnp.float32).astype(jnp.bfloat16)
    grad_attended = grad_attended.reshape(outer_n, length, inner_n, HEADS, HEAD).astype(jnp.float32)
    dprobs = jnp.einsum('aqbhd,akbhd->abhqk', grad_attended, values)
    dvalues = jnp.einsum('abhqk,aqbhd->akbhd', probs_low, grad_attended).astype(jnp.bfloat16)
    dscore = (attn_probs * (dprobs - lax.optimization_barrier(jnp.sum(attn_probs * dprobs, axis=-1, keepdims=True))) * factor).astype(jnp.bfloat16).astype(jnp.float32)
    dquery = jnp.einsum('abhqk,akbhd->aqbhd', dscore, keys_all).astype(jnp.bfloat16)
    dkeys_all = jnp.einsum('abhqk,aqbhd->akbhd', dscore, queries).astype(jnp.bfloat16)
    dpacked = jnp.stack([dquery, dkeys_all, dvalues], axis=3).reshape(-1, 3 * width)
    grad_normed = jnp.dot(dpacked, w_qkv.T, preferred_element_type=jnp.float32).reshape(hidden.shape)
    grad_form = grad_normed * gain_row
    branch = rstd_val * (grad_form - lax.optimization_barrier(jnp.mean(grad_form, axis=-1, keepdims=True)) - normal_form * lax.optimization_barrier(jnp.mean(grad_form * normal_form, axis=-1, keepdims=True)))
    result = (stream.astype(jnp.float32) + branch).astype(jnp.bfloat16)
    term_in = jnp.dot(dpacked.T, flat_normed, preferred_element_type=jnp.float32)
    term_out = jnp.dot(grad_flat.T, attended.reshape(-1, width), preferred_element_type=jnp.float32)
    return (result, jnp.concatenate([term_in, term_out], axis=0))

def run_axis(hidden, stream, axis_id, gain_row, w_qkv, w_out):
    moved = jnp.moveaxis(hidden, axis_id, 2)
    moved_grad = jnp.moveaxis(stream, axis_id, 2)
    shape_all = moved.shape
    length = shape_all[2]
    count_lines = shape_all[0] * shape_all[1]
    per_block = math.gcd(count_lines, max(1, 8192 // length))
    blocked = moved.reshape(count_lines // per_block, per_block, length, 1, C)
    blocked_grad = moved_grad.reshape(count_lines // per_block, per_block, length, 1, C)

    def step_fn(carry, pair):
        result, term = layer_back(pair[0], pair[1], gain_row, w_qkv, w_out)
        return (carry + term, result)
    total_term, results = lax.scan(step_fn, jnp.zeros((4 * C, C), jnp.float32), (blocked, blocked_grad))
    back = jnp.moveaxis(results.reshape(shape_all), 2, axis_id)
    return (back, total_term)

def reference(cotangent, saved_codes, saved_scales, gains, w_qkv, w_out):
    stream = cotangent
    layer_terms = [None, None, None]
    for layer_id in (2, 1, 0):
        hidden = widen(saved_codes[layer_id], saved_scales[layer_id])
        stream, layer_terms[layer_id] = run_axis(hidden, stream, layer_id, gains[layer_id], w_qkv[layer_id], w_out[layer_id])
    whole = jnp.concatenate(layer_terms, axis=1) * (1.0 / math.sqrt(TOKENS))
    return (stream, whole)
```

```python
import functools
import math

import jax
import jax.numpy as jnp
import numpy as np
from jax import lax
from jax.experimental import pallas as pl
from jax.experimental.pallas import tpu as pltpu
from jax.sharding import PartitionSpec as P

C = 384
T = 256
BF = jnp.bfloat16
F32 = jnp.float32
VMEM = 60 * 1024 * 1024


def one_hot_rows(source):
    m = np.zeros((len(source), len(source)), np.float32)
    m[np.arange(len(source)), source] = 1.0
    return m


def token_orders():
    n = np.arange(T)
    to_rows = ((n % 32) // 2) * 16 + 2 * (n // 32) + n % 2
    j, i, r, c = n // 32, (n // 4) % 8, (n // 2) % 2, n % 2
    cols = i * 32 + r * 16 + 2 * j + c
    to_cols = np.zeros((2 * T, T), np.float32)
    to_cols[8 * (n // 4) + n % 4, cols] = 1.0
    from_cols = np.zeros((T, 2 * T), np.float32)
    from_cols[n, 8 * (n // 4) + n % 4] = 1.0
    z, j, r, c = n // 64, (n // 8) % 8, (n // 2) % 4, n % 2
    to_depth = j * 32 + z * 8 + r * 2 + c
    z, r, j, c = n // 64, (n // 16) % 4, (n // 2) % 8, n % 2
    to_home = z * 64 + j * 8 + r * 2 + c
    return [one_hot_rows(to_rows), to_cols, from_cols, one_hot_rows(to_depth), one_hot_rows(to_home)]


def mm(a, b):
    return jnp.dot(a, b, preferred_element_type=F32)


def mm_nt(a, b):
    return lax.dot_general(a, b, (((1,), (1,)), ((), ())), preferred_element_type=F32)


def mm_tn(a, b):
    return lax.dot_general(a, b, (((0,), (0,)), ((), ())), preferred_element_type=F32)


def line_bias(layer):
    q = lax.broadcasted_iota(jnp.int32, (T, T), 0)
    k = lax.broadcasted_iota(jnp.int32, (T, T), 1)
    bits = {2: 16, 1: 1, 0: 63}[layer]
    return jnp.where((q & bits) == (k & bits), 0.0, -1e30).astype(F32)


def head_masks():
    lane = lax.broadcasted_iota(jnp.int32, (1, 128), 1)
    low = jnp.where(lane < 64, 1.0, 0.0).astype(F32)
    return low.astype(BF), (1.0 - low).astype(BF)


def normalise(y):
    y = y.astype(F32)
    rstd = lax.rsqrt(jnp.mean(y * y, axis=-1, keepdims=True) + 1e-05)
    return y * rstd, rstd


def forward(layer, y, gain, w_qkv, probs_ref):
    x_hat, _ = normalise(y)
    normed = (x_hat * gain).astype(BF)
    qkv = mm(normed, w_qkv).astype(BF)
    queries = qkv[:, :C] * jnp.asarray(0.125, BF)
    bias = line_bias(layer)
    masks = head_masks()
    attended = []
    for p in range(3):
        at = slice(128 * p, 128 * p + 128)
        q2, k2, v2 = queries[:, at], qkv[:, C:2 * C][:, at], qkv[:, 2 * C:][:, at]
        out = None
        for side in range(2):
            scores = mm_nt(q2 * masks[side], k2) + bias
            top = jnp.max(scores, axis=-1, keepdims=True)
            e = jnp.exp(scores - top)
            probs = e * (1.0 / jnp.sum(e, axis=-1, keepdims=True))
            low = probs.astype(BF)
            probs_ref[2 * p + side] = low
            part = mm(low, v2 * masks[side])
            out = part if out is None else out + part
        attended.append(out.astype(BF))
    return normed, queries, qkv[:, C:2 * C], qkv[:, 2 * C:], jnp.concatenate(attended, axis=1)


def backward_attention(stream, w_out, queries, keys, values, probs_ref):
    grad_attended = mm_nt(stream, w_out).astype(BF)
    masks = head_masks()
    dq, dk, dv = [], [], []
    for p in range(3):
        at = slice(128 * p, 128 * p + 128)
        q2, k2, v2, g2 = queries[:, at], keys[:, at], values[:, at], grad_attended[:, at]
        sums = None
        for side in range(2):
            low = probs_ref[2 * p + side]
            g = g2 * masks[side]
            probs = low.astype(F32)
            dprobs = mm_nt(g, v2)
            weighted = probs * dprobs
            total = jnp.sum(weighted, axis=-1, keepdims=True)
            dscore = (weighted - probs * total).astype(BF)
            new = (
                mm(dscore, k2 * masks[side]),
                mm_tn(dscore, q2 * masks[side]),
                mm_tn(low, g),
            )
            sums = new if sums is None else tuple(a + b for a, b in zip(sums, new))
        dq.append((sums[0] * 0.125).astype(BF))
        dk.append(sums[1].astype(BF))
        dv.append(sums[2].astype(BF))
    return [jnp.concatenate(d, axis=1) for d in (dq, dk, dv)]


def backward_input(y, stream, gain, w_qkv, parts):
    grad_normed = mm_nt(parts[0], w_qkv[:, :C])
    grad_normed += mm_nt(parts[1], w_qkv[:, C:2 * C])
    grad_normed += mm_nt(parts[2], w_qkv[:, 2 * C:])
    x_hat, rstd = normalise(y)
    d = grad_normed * gain
    branch = rstd * (
        d
        - jnp.mean(d, axis=-1, keepdims=True)
        - x_hat * jnp.mean(d * x_hat, axis=-1, keepdims=True)
    )
    return (stream.astype(F32) + branch).astype(BF)


def weight_terms(parts, normed, stream, attended, keep_ref, send_ref):
    me = lax.axis_index("gy")
    core, x = me % 2, me // 2
    for n, (rows, cols) in enumerate(
        [(parts[0], normed), (parts[1], normed), (parts[2], normed), (stream, attended)]
    ):
        term = mm_tn(rows, cols).astype(BF)
        for j in range(8):
            block = term[48 * j:48 * j + 48]
            slot = (j // 2 + 4 - x) % 4
            at = (slot, slice(48 * n, 48 * n + 48))

            @pl.when((j % 2) == core)
            def _():
                keep_ref[at] = block

            @pl.when((j % 2) != core)
            def _():
                send_ref[at] = block


def place(index, count):
    return pl.ds(pl.multiple_of(count * index, count), count)


def centre_kernel(codes, scales, cot, order, first_ref, *refs):
    token = lax.broadcasted_iota(jnp.int32, (T, 16), 0)
    lane = lax.broadcasted_iota(jnp.int32, (T, 16), 1)
    row_of = jnp.where(token // 16 == lane, 1.0, 0.0).astype(BF)
    col_of = jnp.where(token % 16 == lane, 1.0, 0.0).astype(F32)
    ones = jnp.ones((16, 128), BF)

    def centred(layer):
        blocks = []
        for b in range(3):
            own = (mm(row_of, scales[3 * layer + b]) * col_of).astype(BF)
            blocks.append(codes[layer, :, 128 * b:128 * b + 128].astype(F32) * mm(own, ones))
        h = jnp.concatenate(blocks, axis=1)
        return (h - jnp.mean(h, axis=-1, keepdims=True)).astype(BF)

    first_ref[:, :C] = centred(2)
    first_ref[:, C:] = cot[...]
    both = jnp.concatenate([centred(1), centred(0)], axis=1)
    refs[-1][...] = mm(order[...], both).astype(BF)
    me = lax.axis_index("gy")
    for step in range(8):
        refs[step][...] = refs[-1][place(me ^ step, 32), :]


def column_kernel(x, gains, w_qkv, w_out, order, *refs):
    stream_ref, saved_ref, probs_ref = refs[-3:]
    gain, wq, wo = gains[2:3, :], w_qkv[0], w_out[0]
    y, stream = x[:, :C], x[:, C:]
    normed, queries, keys, values, attended = forward(2, y, gain, wq, probs_ref)
    parts = backward_attention(stream, wo, queries, keys, values, probs_ref)
    new = backward_input(y, stream, gain, wq, parts)
    stream_ref[...] = mm(order[...], new).astype(BF)
    saved_ref[:, :C] = normed
    saved_ref[:, C:2 * C] = attended
    for n in range(3):
        saved_ref[:, (2 + n) * C:(3 + n) * C] = parts[n]


def row_forward_kernel(*refs):
    gains, w_qkv, saved_ref, probs_ref, x_ref = refs[8:]
    me = lax.axis_index("gy")
    for step in range(8):
        x_ref[place(me ^ step, 32), :] = refs[step][...]
    normed, queries, keys, values, attended = forward(1, x_ref[:, :C], gains[1:2, :], w_qkv[0], probs_ref)
    for n, v in enumerate((normed, attended, queries, keys, values)):
        saved_ref[:, n * C:(n + 1) * C] = v


def row_backward_kernel(x, got, saved, probs, gains, w_qkv, w_out, from_cols, order, both_ref, parts_ref, stream_ref):
    stream = mm(from_cols[...], got[...]).astype(BF)
    stream_ref[...] = stream
    parts = backward_attention(
        stream, w_out[0], saved[:, 2 * C:3 * C], saved[:, 3 * C:4 * C], saved[:, 4 * C:], probs
    )
    new = backward_input(x[:, :C], stream, gains[1:2, :], w_qkv[0], parts)
    both_ref[...] = mm(order[...], jnp.concatenate([x[:, C:], new], axis=1)).astype(BF)
    for n in range(3):
        parts_ref[:, n * C:(n + 1) * C] = parts[n]


def column_weight_kernel(saved, stream, keep_ref, send_ref):
    pieces = [saved[:, (2 + n) * C:(3 + n) * C] for n in range(3)]
    weight_terms(pieces, saved[:, :C], stream[...], saved[:, C:2 * C], keep_ref, send_ref)


def row_weight_kernel(saved, parts, stream, keep_ref, send_ref):
    pieces = [parts[:, n * C:(n + 1) * C] for n in range(3)]
    weight_terms(pieces, saved[:, :C], stream[...], saved[:, C:2 * C], keep_ref, send_ref)


def depth_kernel(x, gains, w_qkv, w_out, *refs):
    grad_ref, keep_ref, send_ref, probs_ref = refs[-4:]
    gain, wq, wo = gains[0:1, :], w_qkv[0], w_out[0]
    y, stream = x[:, :C], x[:, C:]
    normed, queries, keys, values, attended = forward(0, y, gain, wq, probs_ref)
    parts = backward_attention(stream, wo, queries, keys, values, probs_ref)
    weight_terms(parts, normed, stream, attended, keep_ref, send_ref)
    grad_ref[...] = backward_input(y, stream, gain, wq, parts)


def home_kernel(x, order, out_ref):
    out_ref[...] = mm(order[...], x[...]).astype(BF)


MAIN = 7 * 128


def sum_kernel(*refs):
    terms, out_ref = refs[:15], refs[15]
    sums = []
    for layer in range(3):
        total = terms[5 * layer][0].astype(F32)
        for term in terms[5 * layer + 1:5 * layer + 5]:
            total = total + term[0].astype(F32)
        sums.append(total.astype(BF))
    total = jnp.concatenate(sums, axis=1)
    row = lax.broadcasted_iota(jnp.int32, (256, 192), 0)
    source = lax.broadcasted_iota(jnp.int32, (256, 192), 1) - 6 * (row // 8)

    def pick(to, of):
        return jnp.where((row % 8 == to) & (source == of), 1.0, 0.0).astype(BF)

    main = jnp.where((row % 8 < 6) & (source == row % 8), 1.0, 0.0).astype(BF)
    out = mm(main, total[:, :MAIN])
    extra = [
        mm(pick(6, q), total[:, MAIN:MAIN + 128]) + mm(pick(7, q), total[:, MAIN + 128:]) for q in range(6)
    ]
    extra.append(jnp.zeros((256, 128), F32))
    out_ref[...] = (out + jnp.concatenate(extra, axis=1)).astype(BF)


def last_sum_kernel(x, out_ref):
    total = x[0].astype(F32)
    for m in range(1, 32):
        total = total + x[m].astype(F32)
    total = total * (1.0 / 256.0)
    out_ref[:, :MAIN] = total[:6, :]
    for q in range(6):
        out_ref[q:q + 1, MAIN:MAIN + 128] = total[6:7, 128 * q:128 * q + 128]
        out_ref[q:q + 1, MAIN + 128:] = total[7:8, 128 * q:128 * q + 128]


def whole(shape):
    return pl.BlockSpec(shape, lambda g: (0,) * len(shape))


def of_layer(array, layer):
    return array, pl.BlockSpec((1,) + array.shape[1:], lambda g: (layer, 0, 0))


def columns(array, first, count):
    return array, pl.BlockSpec((array.shape[0], count), lambda g: (0, first))


def block_zero(array):
    return array, pl.BlockSpec((1,) + array.shape[1:], lambda g: (0, 0, 0))


def after(array):
    return array, pl.BlockSpec(memory_space=pl.ANY)


def call(kernel, ins, outs, scratch=(), flops=5e9):
    ins = [a if isinstance(a, tuple) else (a, whole(a.shape)) for a in ins]
    return pl.pallas_call(
        kernel,
        grid=(1,),
        in_specs=[spec for _, spec in ins],
        out_specs=[whole(s) for s, _ in outs],
        out_shape=[jax.ShapeDtypeStruct(s, d) for s, d in outs],
        scratch_shapes=list(scratch),
        compiler_params=pltpu.CompilerParams(vmem_limit_bytes=VMEM),
        cost_estimate=pl.CostEstimate(flops=int(flops), bytes_accessed=10_000, transcendentals=0),
    )(*[a for a, _ in ins])


CORE_PAIRS = [(j, j ^ 1) for j in range(8)]


def add(a, b):
    return (a.astype(F32) + b.astype(F32)).astype(BF)


def reduce_rows(keep, send):
    first = lax.ppermute(send, "gy", CORE_PAIRS)
    got = [
        lax.ppermute(add(keep[s:s + 1], first[s:s + 1]), "gy", [(j, (j + 2 * s) % 8) for j in range(8)])
        for s in (1, 2, 3)
    ]
    return [keep, first, *got]


def per_device(cotangent, saved_codes, saved_scales, gains, w_qkv, w_out):
    to_rows, to_cols, from_cols, to_depth, to_home = [jnp.asarray(m, BF) for m in token_orders()]
    cot = cotangent.reshape(T, C)
    probs_shape = ((6, T, T), BF)
    tokens = ((T, C), BF)
    pairs = ((T, 2 * C), BF)
    terms = [((4, 192, C), BF), ((4, 192, C), BF)]

    first, *moving = call(
        centre_kernel,
        [saved_codes.reshape(3, T, C), jnp.transpose(saved_scales, (0, 4, 1, 2, 3)).reshape(9, 16, 16), cot, to_rows],
        [pairs] + [((32, 2 * C), BF)] * 8,
        [pltpu.VMEM(*pairs)],
    )
    x2 = lax.all_to_all(first.reshape(8, 32, 2 * C), "gx", 0, 0, tiled=True).reshape(T, 2 * C)
    moving = moving[:1] + [
        lax.ppermute(moving[step], "gy", [(j, j ^ step) for j in range(8)]) for step in range(1, 8)
    ]
    stream2, saved2 = call(
        column_kernel,
        [x2, gains, of_layer(w_qkv, 2), of_layer(w_out, 2), to_cols] + [after(m) for m in moving[1:]],
        [((2 * T, C), BF), ((T, 5 * C), BF)],
        [pltpu.VMEM(*probs_shape)],
    )
    got2 = lax.all_to_all(stream2.reshape(64, 8, C), ("gy", "gx"), 0, 0, tiled=True).reshape(2 * T, C)
    keep2, send2 = call(column_weight_kernel, [saved2, columns(x2, 1, C)], terms)
    saved1, probs1, x1 = call(
        row_forward_kernel,
        moving + [gains, of_layer(w_qkv, 1)],
        [((T, 5 * C), BF), probs_shape, pairs],
    )
    both, parts1, stream2 = call(
        row_backward_kernel,
        [x1, got2, saved1, probs1, gains, of_layer(w_qkv, 1), of_layer(w_out, 1), from_cols, to_depth],
        [pairs, ((T, 3 * C), BF), tokens],
    )
    x0 = lax.all_to_all(both.reshape(4, 64, 2 * C), "gz", 0, 0, tiled=True).reshape(T, 2 * C)
    keep1, send1 = call(row_weight_kernel, [columns(saved1, 0, 2 * C), parts1, stream2], terms)
    sums2 = reduce_rows(keep2, send2)
    sums1 = reduce_rows(keep1, send1)
    grad, keep0, send0 = call(
        depth_kernel,
        [x0, gains, of_layer(w_qkv, 0), of_layer(w_out, 0)] + [after(m) for m in sums2[2:]],
        [tokens] + terms,
        [pltpu.VMEM(*probs_shape)],
    )
    grad = lax.all_to_all(grad.reshape(32, 8, C), ("gz", "gy"), 0, 0, tiled=True).reshape(T, C)
    (rows,) = call(
        sum_kernel,
        [block_zero(m) for m in reduce_rows(keep0, send0) + sums1 + sums2],
        [((T, MAIN), BF)],
    )
    rows = lax.all_to_all(rows.reshape(32, 8, MAIN), ("gz", "gx"), 0, 0, tiled=True)
    (grad,) = call(home_kernel, [grad, to_home], [tokens])
    (weight_grads,) = call(last_sum_kernel, [rows], [((6, 3 * C), F32)])
    return grad.reshape(cotangent.shape), weight_grads


def solution(mesh):
    in_specs = (
        P("gz", "gy", "gx", None),
        P(None, "gz", "gy", "gx", None),
        P(None, "gz", "gy", "gx", None),
        P(),
        P(),
        P(),
    )
    out_specs = (P("gz", "gy", "gx", None), P(("gz", "gy", "gx"), None))
    return jax.shard_map(
        per_device, mesh=mesh, in_specs=in_specs, out_specs=out_specs, check_vma=False
    )
```

```python
import functools
import math

import jax
import jax.numpy as jnp
import numpy as np
from jax import lax
from jax.experimental import pallas as pl
from jax.experimental.pallas import tpu as pltpu
from jax.sharding import PartitionSpec as P

C = 384
T = 256
BF = jnp.bfloat16
F32 = jnp.float32
VMEM = 60 * 1024 * 1024


def one_hot_rows(source):
    m = np.zeros((len(source), len(source)), np.float32)
    m[np.arange(len(source)), source] = 1.0
    return m


def token_orders():
    n = np.arange(T)
    to_rows = ((n % 32) // 2) * 16 + 2 * (n // 32) + n % 2
    j, i, r, c = n // 32, (n // 4) % 8, (n // 2) % 2, n % 2
    cols = i * 32 + r * 16 + 2 * j + c
    to_cols = np.zeros((4 * T, T), np.float32)
    from_cols = np.zeros((T, 4 * T), np.float32)
    for g in range(3):
        at = 16 * (n // 4) + 4 * g + n % 4
        to_cols[at, cols] = 1.0
        from_cols[n, at] = 1.0
    z, j, r, c = n // 64, (n // 8) % 8, (n // 2) % 4, n % 2
    to_depth = j * 32 + z * 8 + r * 2 + c
    z, r, j, c = n // 64, (n // 16) % 4, (n // 2) % 8, n % 2
    to_home = z * 64 + j * 8 + r * 2 + c
    return [one_hot_rows(to_rows), to_cols, from_cols, one_hot_rows(to_depth), one_hot_rows(to_home)]


def mm(a, b):
    return jnp.dot(a, b, preferred_element_type=F32)


def mm_nt(a, b):
    return lax.dot_general(a, b, (((1,), (1,)), ((), ())), preferred_element_type=F32)


def mm_tn(a, b):
    return lax.dot_general(a, b, (((0,), (0,)), ((), ())), preferred_element_type=F32)


def line_bias(layer):
    q = lax.broadcasted_iota(jnp.int32, (T, T), 0)
    k = lax.broadcasted_iota(jnp.int32, (T, T), 1)
    bits = {2: 16, 1: 1, 0: 63}[layer]
    return jnp.where((q & bits) == (k & bits), 0.0, -1e30).astype(F32)


def head_masks():
    lane = lax.broadcasted_iota(jnp.int32, (1, 128), 1)
    low = jnp.where(lane < 64, 1.0, 0.0).astype(F32)
    return low.astype(BF), (1.0 - low).astype(BF)


def normalise(y):
    y = y.astype(F32)
    rstd = lax.rsqrt(jnp.mean(y * y, axis=-1, keepdims=True) + 1e-05)
    return y * rstd, rstd


def forward(layer, y, gain, w_qkv, probs_ref):
    x_hat, _ = normalise(y)
    normed = (x_hat * gain).astype(BF)
    qkv = mm(normed, w_qkv).astype(BF)
    queries = qkv[:, :C] * jnp.asarray(0.125, BF)
    bias = line_bias(layer)
    masks = head_masks()
    attended = []
    for p in range(3):
        at = slice(128 * p, 128 * p + 128)
        q2, k2, v2 = queries[:, at], qkv[:, C:2 * C][:, at], qkv[:, 2 * C:][:, at]
        out = None
        for side in range(2):
            scores = mm_nt(q2 * masks[side], k2) + bias
            top = jnp.max(scores, axis=-1, keepdims=True)
            e = jnp.exp(scores - top)
            probs = e * (1.0 / jnp.sum(e, axis=-1, keepdims=True))
            low = probs.astype(BF)
            probs_ref[2 * p + side] = low
            part = mm(low, v2 * masks[side])
            out = part if out is None else out + part
        attended.append(out.astype(BF))
    return normed, queries, qkv[:, C:2 * C], qkv[:, 2 * C:], jnp.concatenate(attended, axis=1)


def backward_attention(stream, w_out, queries, keys, values, probs_ref):
    grad_attended = mm_nt(stream, w_out).astype(BF)
    masks = head_masks()
    dq, dk, dv = [], [], []
    for p in range(3):
        at = slice(128 * p, 128 * p + 128)
        q2, k2, v2, g2 = queries[:, at], keys[:, at], values[:, at], grad_attended[:, at]
        sums = None
        for side in range(2):
            low = probs_ref[2 * p + side]
            g = g2 * masks[side]
            probs = low.astype(F32)
            dprobs = mm_nt(g, v2)
            weighted = probs * dprobs
            total = jnp.sum(weighted, axis=-1, keepdims=True)
            dscore = (weighted - probs * total).astype(BF)
            new = (
                mm(dscore, k2 * masks[side]),
                mm_tn(dscore, q2 * masks[side]),
                mm_tn(low, g),
            )
            sums = new if sums is None else tuple(a + b for a, b in zip(sums, new))
        dq.append((sums[0] * 0.125).astype(BF))
        dk.append(sums[1].astype(BF))
        dv.append(sums[2].astype(BF))
    return [jnp.concatenate(d, axis=1) for d in (dq, dk, dv)]


def backward_input(y, stream, gain, w_qkv, parts):
    grad_normed = mm_nt(parts[0], w_qkv[:, :C])
    grad_normed += mm_nt(parts[1], w_qkv[:, C:2 * C])
    grad_normed += mm_nt(parts[2], w_qkv[:, 2 * C:])
    x_hat, rstd = normalise(y)
    d = grad_normed * gain
    branch = rstd * (
        d
        - jnp.mean(d, axis=-1, keepdims=True)
        - x_hat * jnp.mean(d * x_hat, axis=-1, keepdims=True)
    )
    return (stream.astype(F32) + branch).astype(BF)


def weight_terms(parts, normed, stream, attended, keep_ref, send_ref):
    me = lax.axis_index("gy")
    core, x = me % 2, me // 2
    for n, (rows, cols) in enumerate(
        [(parts[0], normed), (parts[1], normed), (parts[2], normed), (stream, attended)]
    ):
        term = mm_tn(rows, cols).astype(BF)
        for j in range(8):
            block = term[48 * j:48 * j + 48]
            slot = (j // 2 + 4 - x) % 4
            at = (slot, slice(48 * n, 48 * n + 48))

            @pl.when((j % 2) == core)
            def _():
                keep_ref[at] = block

            @pl.when((j % 2) != core)
            def _():
                send_ref[at] = block


def centred(codes, scales):
    token = lax.broadcasted_iota(jnp.int32, (T, 16), 0)
    lane = lax.broadcasted_iota(jnp.int32, (T, 16), 1)
    row_of = jnp.where(token // 16 == lane, 1.0, 0.0).astype(BF)
    col_of = jnp.where(token % 16 == lane, 1.0, 0.0).astype(F32)
    ones = jnp.ones((16, 128), BF)
    blocks = []
    for b in range(3):
        own = (mm(row_of, scales[b]) * col_of).astype(BF)
        blocks.append(codes[:, 128 * b:128 * b + 128].astype(F32) * mm(own, ones))
    h = jnp.concatenate(blocks, axis=1)
    return (h - jnp.mean(h, axis=-1, keepdims=True)).astype(BF)


def first_kernel(codes, scales, cot, out_ref):
    out_ref[:, :C] = centred(codes[0], scales)
    out_ref[:, C:] = cot[...]


def second_kernel(codes, scales, order, out_ref):
    both = jnp.concatenate([centred(codes[1], scales[3:]), centred(codes[0], scales[:3])], axis=1)
    out_ref[...] = mm(order[...], both).astype(BF)


def message_group():
    return lax.broadcasted_iota(jnp.int32, (4 * T, 128), 0) % 16 // 4


def column_kernel(x, gains, w_qkv, w_out, order, *refs):
    stream_ref, saved_ref, probs_ref = refs[-3:]
    gain, wq, wo = gains[2:3, :], w_qkv[0], w_out[0]
    y, stream = x[:, :C], x[:, C:]
    normed, queries, keys, values, attended = forward(2, y, gain, wq, probs_ref)
    parts = backward_attention(stream, wo, queries, keys, values, probs_ref)
    new = backward_input(y, stream, gain, wq, parts)
    wide = mm(order[...], new)
    group = message_group()
    stream_ref[...] = jnp.where(
        group == 0, wide[:, :128], jnp.where(group == 1, wide[:, 128:256], wide[:, 256:])
    ).astype(BF)
    saved_ref[:, :C] = normed
    saved_ref[:, C:2 * C] = attended
    for n in range(3):
        saved_ref[:, (2 + n) * C:(3 + n) * C] = parts[n]


def row_forward_kernel(x, gains, w_qkv, saved_ref, probs_ref):
    normed, queries, keys, values, attended = forward(1, x[...], gains[1:2, :], w_qkv[0], probs_ref)
    for n, v in enumerate((normed, attended, queries, keys, values)):
        saved_ref[:, n * C:(n + 1) * C] = v


def row_backward_kernel(x, got, saved, probs, gains, w_qkv, w_out, from_cols, order, both_ref, parts_ref, stream_ref):
    group = message_group()
    arrived = got[...].astype(F32)
    wide = jnp.concatenate([jnp.where(group == g, arrived, 0.0).astype(BF) for g in range(3)], axis=1)
    stream = mm(from_cols[...], wide).astype(BF)
    stream_ref[...] = stream
    parts = backward_attention(
        stream, w_out[0], saved[:, 2 * C:3 * C], saved[:, 3 * C:4 * C], saved[:, 4 * C:], probs
    )
    new = backward_input(x[:, :C], stream, gains[1:2, :], w_qkv[0], parts)
    both_ref[...] = mm(order[...], jnp.concatenate([x[:, C:], new], axis=1)).astype(BF)
    for n in range(3):
        parts_ref[:, n * C:(n + 1) * C] = parts[n]


def column_weight_kernel(saved, stream, keep_ref, send_ref):
    pieces = [saved[:, (2 + n) * C:(3 + n) * C] for n in range(3)]
    weight_terms(pieces, saved[:, :C], stream[...], saved[:, C:2 * C], keep_ref, send_ref)


def row_weight_kernel(saved, parts, stream, keep_ref, send_ref):
    pieces = [parts[:, n * C:(n + 1) * C] for n in range(3)]
    weight_terms(pieces, saved[:, :C], stream[...], saved[:, C:2 * C], keep_ref, send_ref)


def depth_kernel(x, gains, w_qkv, w_out, *refs):
    grad_ref, keep_ref, send_ref, probs_ref = refs[-4:]
    gain, wq, wo = gains[0:1, :], w_qkv[0], w_out[0]
    y, stream = x[:, :C], x[:, C:]
    normed, queries, keys, values, attended = forward(0, y, gain, wq, probs_ref)
    parts = backward_attention(stream, wo, queries, keys, values, probs_ref)
    weight_terms(parts, normed, stream, attended, keep_ref, send_ref)
    grad_ref[...] = backward_input(y, stream, gain, wq, parts)


def home_kernel(x, order, out_ref):
    out_ref[...] = mm(order[...], x[...]).astype(BF)


MAIN = 7 * 128


def sum_kernel(*refs):
    terms, out_ref = refs[:15], refs[15]
    sums = []
    for layer in range(3):
        total = terms[5 * layer][0].astype(F32)
        for term in terms[5 * layer + 1:5 * layer + 5]:
            total = total + term[0].astype(F32)
        sums.append(total.astype(BF))
    total = jnp.concatenate(sums, axis=1)
    row = lax.broadcasted_iota(jnp.int32, (256, 192), 0)
    source = lax.broadcasted_iota(jnp.int32, (256, 192), 1) - 6 * (row // 8)

    def pick(to, of):
        return jnp.where((row % 8 == to) & (source == of), 1.0, 0.0).astype(BF)

    main = jnp.where((row % 8 < 6) & (source == row % 8), 1.0, 0.0).astype(BF)
    out = mm(main, total[:, :MAIN])
    extra = [
        mm(pick(6, q), total[:, MAIN:MAIN + 128]) + mm(pick(7, q), total[:, MAIN + 128:]) for q in range(6)
    ]
    extra.append(jnp.zeros((256, 128), F32))
    out_ref[...] = (out + jnp.concatenate(extra, axis=1)).astype(BF)


def last_sum_kernel(x, out_ref):
    total = x[0].astype(F32)
    for m in range(1, 32):
        total = total + x[m].astype(F32)
    total = total * (1.0 / 256.0)
    out_ref[:, :MAIN] = total[:6, :]
    for q in range(6):
        out_ref[q:q + 1, MAIN:MAIN + 128] = total[6:7, 128 * q:128 * q + 128]
        out_ref[q:q + 1, MAIN + 128:] = total[7:8, 128 * q:128 * q + 128]


def whole(shape):
    return pl.BlockSpec(shape, lambda g: (0,) * len(shape))


def of_layer(array, layer):
    return array, pl.BlockSpec((1,) + array.shape[1:], lambda g: (layer, 0, 0))


def rows_of(array, first, count):
    return array, pl.BlockSpec((count,) + array.shape[1:], lambda g: (first, 0, 0))


def columns(array, first, count):
    return array, pl.BlockSpec((array.shape[0], count), lambda g: (0, first))


def block_zero(array):
    return array, pl.BlockSpec((1,) + array.shape[1:], lambda g: (0, 0, 0))


def after(array):
    return array, pl.BlockSpec(memory_space=pl.ANY)


def call(kernel, ins, outs, scratch=(), flops=5e9, vmem=VMEM):
    ins = [a if isinstance(a, tuple) else (a, whole(a.shape)) for a in ins]
    return pl.pallas_call(
        kernel,
        grid=(1,),
        in_specs=[spec for _, spec in ins],
        out_specs=[whole(s) for s, _ in outs],
        out_shape=[jax.ShapeDtypeStruct(s, d) for s, d in outs],
        scratch_shapes=list(scratch),
        compiler_params=pltpu.CompilerParams(vmem_limit_bytes=vmem),
        cost_estimate=pl.CostEstimate(flops=int(flops), bytes_accessed=10_000, transcendentals=0),
    )(*[a for a, _ in ins])


CORE_PAIRS = [(j, j ^ 1) for j in range(8)]


def add(a, b):
    return (a.astype(F32) + b.astype(F32)).astype(BF)


def reduce_rows(keep, send):
    first = lax.ppermute(send, "gy", CORE_PAIRS)
    got = [
        lax.ppermute(add(keep[s:s + 1], first[s:s + 1]), "gy", [(j, (j + 2 * s) % 8) for j in range(8)])
        for s in (1, 2, 3)
    ]
    return [keep, first, *got]


def per_device(cotangent, saved_codes, saved_scales, gains, w_qkv, w_out):
    to_rows, to_cols, from_cols, to_depth, to_home = [jnp.asarray(m, BF) for m in token_orders()]
    cot = cotangent.reshape(T, C)
    probs_shape = ((6, T, T), BF)
    tokens = ((T, C), BF)
    pairs = ((T, 2 * C), BF)
    terms = [((4, 192, C), BF), ((4, 192, C), BF)]

    codes = saved_codes.reshape(3, T, C)
    scales = jnp.transpose(saved_scales, (0, 4, 1, 2, 3)).reshape(9, 16, 16)
    (first,) = call(first_kernel, [of_layer(codes, 2), rows_of(scales, 2, 3), cot], [pairs])
    x2 = lax.all_to_all(first.reshape(8, 32, 2 * C), "gx", 0, 0, tiled=True).reshape(T, 2 * C)
    (second,) = call(second_kernel, [rows_of(codes, 0, 2), rows_of(scales, 0, 6), to_rows], [pairs])
    x1 = lax.all_to_all(second.reshape(8, 32, 2 * C), "gy", 0, 0, tiled=True).reshape(T, 2 * C)
    stream2, saved2 = call(
        column_kernel,
        [x2, gains, of_layer(w_qkv, 2), of_layer(w_out, 2), to_cols],
        [((4 * T, 128), BF), ((T, 5 * C), BF)],
        [pltpu.VMEM(*probs_shape)],
    )
    got2 = lax.all_to_all(stream2.reshape(64, 16, 128), ("gy", "gx"), 0, 0, tiled=True).reshape(4 * T, 128)
    keep2, send2 = call(column_weight_kernel, [saved2, columns(x2, 1, C)], terms)
    saved1, probs1 = call(
        row_forward_kernel,
        [columns(x1, 0, C), gains, of_layer(w_qkv, 1)],
        [((T, 5 * C), BF), probs_shape],
    )
    both, parts1, stream2 = call(
        row_backward_kernel,
        [x1, got2, saved1, probs1, gains, of_layer(w_qkv, 1), of_layer(w_out, 1), from_cols, to_depth],
        [pairs, ((T, 3 * C), BF), tokens],
    )
    x0 = lax.all_to_all(both.reshape(4, 64, 2 * C), "gz", 0, 0, tiled=True).reshape(T, 2 * C)
    keep1, send1 = call(row_weight_kernel, [columns(saved1, 0, 2 * C), parts1, stream2], terms)
    sums2 = reduce_rows(keep2, send2)
    sums1 = reduce_rows(keep1, send1)
    grad, keep0, send0 = call(
        depth_kernel,
        [x0, gains, of_layer(w_qkv, 0), of_layer(w_out, 0)] + [after(m) for m in sums2[2:]],
        [tokens] + terms,
        [pltpu.VMEM(*probs_shape)],
    )
    grad = lax.all_to_all(grad.reshape(32, 8, C), ("gz", "gy"), 0, 0, tiled=True).reshape(T, C)
    (rows,) = call(
        sum_kernel,
        [block_zero(m) for m in reduce_rows(keep0, send0) + sums1 + sums2],
        [((T, MAIN), BF)],
    )
    rows = lax.all_to_all(rows.reshape(32, 8, MAIN), ("gz", "gx"), 0, 0, tiled=True)
    (grad,) = call(home_kernel, [grad, to_home], [tokens])
    (weight_grads,) = call(last_sum_kernel, [rows], [((6, 3 * C), F32)], vmem=16 << 20)
    return grad.reshape(cotangent.shape), weight_grads


def solution(mesh):
    in_specs = (
        P("gz", "gy", "gx", None),
        P(None, "gz", "gy", "gx", None),
        P(None, "gz", "gy", "gx", None),
        P(),
        P(),
        P(),
    )
    out_specs = (P("gz", "gy", "gx", None), P(("gz", "gy", "gx"), None))
    return jax.shard_map(
        per_device, mesh=mesh, in_specs=in_specs, out_specs=out_specs, check_vma=False
    )
```

```python
import functools
import math

import jax
import jax.numpy as jnp
import numpy as np
from jax import lax
from jax.experimental import pallas as pl
from jax.experimental.pallas import tpu as pltpu
from jax.sharding import PartitionSpec as P

C = 384
T = 256
BF = jnp.bfloat16
F32 = jnp.float32
VMEM = 60 * 1024 * 1024


def one_hot_rows(source):
    m = np.zeros((len(source), len(source)), np.float32)
    m[np.arange(len(source)), source] = 1.0
    return m


def token_orders():
    n = np.arange(T)
    to_rows = ((n % 32) // 2) * 16 + 2 * (n // 32) + n % 2
    j, i, r, c = n // 32, (n // 4) % 8, (n // 2) % 2, n % 2
    cols = i * 32 + r * 16 + 2 * j + c
    to_cols = np.zeros((4 * T, T), np.float32)
    from_cols = np.zeros((T, 4 * T), np.float32)
    for g in range(3):
        at = 16 * (n // 4) + 4 * g + n % 4
        to_cols[at, cols] = 1.0
        from_cols[n, at] = 1.0
    z, j, r, c = n // 64, (n // 8) % 8, (n // 2) % 4, n % 2
    to_depth = j * 32 + z * 8 + r * 2 + c
    z, r, j, c = n // 64, (n // 16) % 4, (n // 2) % 8, n % 2
    to_home = z * 64 + j * 8 + r * 2 + c
    return [one_hot_rows(to_rows), to_cols, from_cols, one_hot_rows(to_depth), one_hot_rows(to_home)]


def mm(a, b):
    return jnp.dot(a, b, preferred_element_type=F32)


def mm_nt(a, b):
    return lax.dot_general(a, b, (((1,), (1,)), ((), ())), preferred_element_type=F32)


def mm_tn(a, b):
    return lax.dot_general(a, b, (((0,), (0,)), ((), ())), preferred_element_type=F32)


def line_bias(layer):
    q = lax.broadcasted_iota(jnp.int32, (T, T), 0)
    k = lax.broadcasted_iota(jnp.int32, (T, T), 1)
    bits = {2: 16, 1: 1, 0: 63}[layer]
    return jnp.where((q & bits) == (k & bits), 0.0, -1e30).astype(F32)


def head_masks():
    lane = lax.broadcasted_iota(jnp.int32, (1, 128), 1)
    low = jnp.where(lane < 64, 1.0, 0.0).astype(F32)
    return low.astype(BF), (1.0 - low).astype(BF)


def pair(a, p):
    return a[:, 128 * p:128 * p + 128]


def low_lanes():
    return lax.broadcasted_iota(jnp.int32, (T, 128), 1) < 64


def normalise(y):
    y = y.astype(F32)
    rstd = lax.rsqrt(jnp.mean(y * y, axis=-1, keepdims=True) + 1e-05)
    return y * rstd, rstd


def forward(layer, y, gain, w_qkv, probs_ref):
    x_hat, _ = normalise(y)
    normed = (x_hat * gain).astype(BF)
    qkv = mm(normed, w_qkv).astype(BF)
    queries = qkv[:, :C] * jnp.asarray(0.125, BF)
    bias = line_bias(layer)
    masks = head_masks()
    keys, values = qkv[:, C:2 * C], qkv[:, 2 * C:]
    scores = [mm_nt(pair(queries, n // 2) * masks[n % 2], pair(keys, n // 2)) + bias for n in range(6)]
    es = [jnp.exp(s - jnp.max(s, axis=-1, keepdims=True)) for s in scores]
    lows = [(e * (1.0 / jnp.sum(e, axis=-1, keepdims=True))).astype(BF) for e in es]
    attended = []
    for p in range(3):
        probs_ref[2 * p] = lows[2 * p]
        probs_ref[2 * p + 1] = lows[2 * p + 1]
        v2 = pair(values, p)
        attended.append(jnp.where(low_lanes(), mm(lows[2 * p], v2), mm(lows[2 * p + 1], v2)).astype(BF))
    return normed, queries, qkv[:, C:2 * C], qkv[:, 2 * C:], jnp.concatenate(attended, axis=1)


def backward_attention(stream, w_out, queries, keys, values, probs_ref):
    grad_attended = mm_nt(stream, w_out).astype(BF)
    masks = head_masks()
    gs = [pair(grad_attended, n // 2) * masks[n % 2] for n in range(6)]
    dprobs = [mm_nt(gs[n], pair(values, n // 2)) for n in range(6)]
    dscores = []
    for n in range(6):
        probs = probs_ref[n].astype(F32)
        weighted = probs * dprobs[n]
        total = jnp.sum(weighted, axis=-1, keepdims=True)
        dscores.append((weighted - probs * total).astype(BF))
    dq, dk, dv = [], [], []
    for p in range(3):
        k2, q2 = pair(keys, p), pair(queries, p)
        a, b = 2 * p, 2 * p + 1
        g2 = pair(grad_attended, p)
        low = low_lanes()
        dq.append((jnp.where(low, mm(dscores[a], k2), mm(dscores[b], k2)) * 0.125).astype(BF))
        dk.append(jnp.where(low, mm_tn(dscores[a], q2), mm_tn(dscores[b], q2)).astype(BF))
        dv.append(jnp.where(low, mm_tn(probs_ref[a], g2), mm_tn(probs_ref[b], g2)).astype(BF))
    return [jnp.concatenate(d, axis=1) for d in (dq, dk, dv)]


def backward_input(y, stream, gain, w_qkv, parts):
    grad_normed = mm_nt(parts[0], w_qkv[:, :C])
    grad_normed += mm_nt(parts[1], w_qkv[:, C:2 * C])
    grad_normed += mm_nt(parts[2], w_qkv[:, 2 * C:])
    x_hat, rstd = normalise(y)
    d = grad_normed * gain
    branch = rstd * (
        d
        - jnp.mean(d, axis=-1, keepdims=True)
        - x_hat * jnp.mean(d * x_hat, axis=-1, keepdims=True)
    )
    return (stream.astype(F32) + branch).astype(BF)


def weight_terms(parts, normed, stream, attended, keep_ref, send_ref):
    me = lax.axis_index("gy")
    core, x = me % 2, me // 2
    for n, (rows, cols) in enumerate(
        [(parts[0], normed), (parts[1], normed), (parts[2], normed), (stream, attended)]
    ):
        term = mm_tn(rows, cols).astype(BF)
        for j in range(8):
            block = term[48 * j:48 * j + 48]
            slot = (j // 2 + 4 - x) % 4
            at = (slot, slice(48 * n, 48 * n + 48))

            @pl.when((j % 2) == core)
            def _():
                keep_ref[at] = block

            @pl.when((j % 2) != core)
            def _():
                send_ref[at] = block


def centred(codes, scales):
    token = lax.broadcasted_iota(jnp.int32, (T, 16), 0)
    lane = lax.broadcasted_iota(jnp.int32, (T, 16), 1)
    row_of = jnp.where(token // 16 == lane, 1.0, 0.0).astype(BF)
    col_of = jnp.where(token % 16 == lane, 1.0, 0.0).astype(F32)
    ones = jnp.ones((16, 128), BF)
    blocks = []
    for b in range(3):
        own = (mm(row_of, scales[b]) * col_of).astype(BF)
        blocks.append(codes[:, 128 * b:128 * b + 128].astype(F32) * mm(own, ones))
    h = jnp.concatenate(blocks, axis=1)
    return (h - jnp.mean(h, axis=-1, keepdims=True)).astype(BF)


def first_kernel(codes, scales, cot, out_ref):
    out_ref[:, :C] = centred(codes[0], scales)
    out_ref[:, C:] = cot[...]


def second_kernel(codes, scales, order, out_ref):
    both = jnp.concatenate([centred(codes[1], scales[3:]), centred(codes[0], scales[:3])], axis=1)
    out_ref[...] = mm(order[...], both).astype(BF)


def message_group():
    return lax.broadcasted_iota(jnp.int32, (4 * T, 128), 0) % 16 // 4


def column_kernel(x, gains, w_qkv, w_out, order, *refs):
    stream_ref, saved_ref, probs_ref = refs[-3:]
    gain, wq, wo = gains[2:3, :], w_qkv[0], w_out[0]
    y, stream = x[:, :C], x[:, C:]
    normed, queries, keys, values, attended = forward(2, y, gain, wq, probs_ref)
    parts = backward_attention(stream, wo, queries, keys, values, probs_ref)
    new = backward_input(y, stream, gain, wq, parts)
    wide = mm(order[...], new)
    group = message_group()
    stream_ref[...] = jnp.where(
        group == 0, wide[:, :128], jnp.where(group == 1, wide[:, 128:256], wide[:, 256:])
    ).astype(BF)
    saved_ref[:, :C] = normed
    saved_ref[:, C:2 * C] = attended
    for n in range(3):
        saved_ref[:, (2 + n) * C:(3 + n) * C] = parts[n]


def row_forward_kernel(x, gains, w_qkv, saved_ref, packed_ref, probs_ref):
    normed, queries, keys, values, attended = forward(1, x[...], gains[1:2, :], w_qkv[0], probs_ref)
    saved_ref[:, :C] = normed
    saved_ref[:, C:] = attended
    for n, v in enumerate((queries, keys, values)):
        packed_ref[:, n * C:(n + 1) * C] = v


def row_backward_kernel(x, got, packed, probs, gains, w_qkv, w_out, from_cols, order, both_ref, parts_ref, stream_ref):
    group = message_group()
    arrived = got[...].astype(F32)
    wide = jnp.concatenate([jnp.where(group == g, arrived, 0.0).astype(BF) for g in range(3)], axis=1)
    stream = mm(from_cols[...], wide).astype(BF)
    stream_ref[...] = stream
    parts = backward_attention(
        stream, w_out[0], packed[:, :C], packed[:, C:2 * C], packed[:, 2 * C:], probs
    )
    new = backward_input(x[:, :C], stream, gains[1:2, :], w_qkv[0], parts)
    both_ref[...] = mm(order[...], jnp.concatenate([x[:, C:], new], axis=1)).astype(BF)
    for n in range(3):
        parts_ref[:, n * C:(n + 1) * C] = parts[n]


def column_weight_kernel(saved, stream, keep_ref, send_ref):
    pieces = [saved[:, (2 + n) * C:(3 + n) * C] for n in range(3)]
    weight_terms(pieces, saved[:, :C], stream[...], saved[:, C:2 * C], keep_ref, send_ref)


def row_weight_kernel(saved, parts, stream, keep_ref, send_ref):
    pieces = [parts[:, n * C:(n + 1) * C] for n in range(3)]
    weight_terms(pieces, saved[:, :C], stream[...], saved[:, C:2 * C], keep_ref, send_ref)


def depth_kernel(x, gains, w_qkv, w_out, *refs):
    grad_ref, keep_ref, send_ref, probs_ref = refs[-4:]
    gain, wq, wo = gains[0:1, :], w_qkv[0], w_out[0]
    y, stream = x[:, :C], x[:, C:]
    normed, queries, keys, values, attended = forward(0, y, gain, wq, probs_ref)
    parts = backward_attention(stream, wo, queries, keys, values, probs_ref)
    weight_terms(parts, normed, stream, attended, keep_ref, send_ref)
    grad_ref[...] = backward_input(y, stream, gain, wq, parts)


def home_kernel(x, order, out_ref):
    out_ref[...] = mm(order[...], x[...]).astype(BF)


MAIN = 7 * 128


def sum_kernel(*refs):
    terms, out_ref = refs[:15], refs[15]
    sums = []
    for layer in range(3):
        total = terms[5 * layer][0].astype(F32)
        for term in terms[5 * layer + 1:5 * layer + 5]:
            total = total + term[0].astype(F32)
        sums.append(total.astype(BF))
    total = jnp.concatenate(sums, axis=1)
    row = lax.broadcasted_iota(jnp.int32, (256, 192), 0)
    source = lax.broadcasted_iota(jnp.int32, (256, 192), 1) - 6 * (row // 8)

    def pick(to, of):
        return jnp.where((row % 8 == to) & (source == of), 1.0, 0.0).astype(BF)

    main = jnp.where((row % 8 < 6) & (source == row % 8), 1.0, 0.0).astype(BF)
    out = mm(main, total[:, :MAIN])
    extra = [
        mm(pick(6, q), total[:, MAIN:MAIN + 128]) + mm(pick(7, q), total[:, MAIN + 128:]) for q in range(6)
    ]
    extra.append(jnp.zeros((256, 128), F32))
    out_ref[...] = (out + jnp.concatenate(extra, axis=1)).astype(BF)


def last_sum_kernel(x, out_ref):
    total = x[0].astype(F32)
    for m in range(1, 32):
        total = total + x[m].astype(F32)
    total = total * (1.0 / 256.0)
    out_ref[:, :MAIN] = total[:6, :]
    for q in range(6):
        out_ref[q:q + 1, MAIN:MAIN + 128] = total[6:7, 128 * q:128 * q + 128]
        out_ref[q:q + 1, MAIN + 128:] = total[7:8, 128 * q:128 * q + 128]


def whole(shape):
    return pl.BlockSpec(shape, lambda g: (0,) * len(shape))


def of_layer(array, layer):
    return array, pl.BlockSpec((1,) + array.shape[1:], lambda g: (layer, 0, 0))


def rows_of(array, first, count):
    return array, pl.BlockSpec((count,) + array.shape[1:], lambda g: (first, 0, 0))


def columns(array, first, count):
    return array, pl.BlockSpec((array.shape[0], count), lambda g: (0, first))


def block_zero(array):
    return array, pl.BlockSpec((1,) + array.shape[1:], lambda g: (0, 0, 0))


def after(array):
    return array, pl.BlockSpec(memory_space=pl.ANY)


def call(kernel, ins, outs, scratch=(), flops=5e9, vmem=VMEM):
    ins = [a if isinstance(a, tuple) else (a, whole(a.shape)) for a in ins]
    return pl.pallas_call(
        kernel,
        grid=(1,),
        in_specs=[spec for _, spec in ins],
        out_specs=[whole(s) for s, _ in outs],
        out_shape=[jax.ShapeDtypeStruct(s, d) for s, d in outs],
        scratch_shapes=list(scratch),
        compiler_params=pltpu.CompilerParams(vmem_limit_bytes=vmem),
        cost_estimate=pl.CostEstimate(flops=int(flops), bytes_accessed=10_000, transcendentals=0),
    )(*[a for a, _ in ins])


CORE_PAIRS = [(j, j ^ 1) for j in range(8)]


def add(a, b):
    return (a.astype(F32) + b.astype(F32)).astype(BF)


def reduce_rows(keep, send):
    first = lax.ppermute(send, "gy", CORE_PAIRS)
    got = [
        lax.ppermute(add(keep[s:s + 1], first[s:s + 1]), "gy", [(j, (j + 2 * s) % 8) for j in range(8)])
        for s in (1, 2, 3)
    ]
    return [keep, first, *got]


def per_device(cotangent, saved_codes, saved_scales, gains, w_qkv, w_out):
    to_rows, to_cols, from_cols, to_depth, to_home = [jnp.asarray(m, BF) for m in token_orders()]
    cot = cotangent.reshape(T, C)
    probs_shape = ((6, T, T), BF)
    tokens = ((T, C), BF)
    pairs = ((T, 2 * C), BF)
    terms = [((4, 192, C), BF), ((4, 192, C), BF)]

    codes = saved_codes.reshape(3, T, C)
    scales = jnp.transpose(saved_scales, (0, 4, 1, 2, 3)).reshape(9, 16, 16)
    (first,) = call(first_kernel, [of_layer(codes, 2), rows_of(scales, 2, 3), cot], [pairs])
    x2 = lax.all_to_all(first.reshape(8, 32, 2 * C), "gx", 0, 0, tiled=True).reshape(T, 2 * C)
    (second,) = call(second_kernel, [rows_of(codes, 0, 2), rows_of(scales, 0, 6), to_rows], [pairs])
    x1 = lax.all_to_all(second.reshape(8, 32, 2 * C), "gy", 0, 0, tiled=True).reshape(T, 2 * C)
    stream2, saved2 = call(
        column_kernel,
        [x2, gains, of_layer(w_qkv, 2), of_layer(w_out, 2), to_cols],
        [((4 * T, 128), BF), ((T, 5 * C), BF)],
        [pltpu.VMEM(*probs_shape)],
    )
    got2 = lax.all_to_all(stream2.reshape(64, 16, 128), ("gy", "gx"), 0, 0, tiled=True).reshape(4 * T, 128)
    keep2, send2 = call(column_weight_kernel, [saved2, columns(x2, 1, C)], terms)
    saved1, packed1, probs1 = call(
        row_forward_kernel,
        [columns(x1, 0, C), gains, of_layer(w_qkv, 1)],
        [pairs, ((T, 3 * C), BF), probs_shape],
    )
    both, parts1, stream2 = call(
        row_backward_kernel,
        [x1, got2, packed1, probs1, gains, of_layer(w_qkv, 1), of_layer(w_out, 1), from_cols, to_depth],
        [pairs, ((T, 3 * C), BF), tokens],
    )
    x0 = lax.all_to_all(both.reshape(4, 64, 2 * C), "gz", 0, 0, tiled=True).reshape(T, 2 * C)
    keep1, send1 = call(row_weight_kernel, [saved1, parts1, stream2], terms)
    sums2 = reduce_rows(keep2, send2)
    sums1 = reduce_rows(keep1, send1)
    grad, keep0, send0 = call(
        depth_kernel,
        [x0, gains, of_layer(w_qkv, 0), of_layer(w_out, 0)] + [after(m) for m in sums2[2:]],
        [tokens] + terms,
        [pltpu.VMEM(*probs_shape)],
    )
    grad = lax.all_to_all(grad.reshape(32, 8, C), ("gz", "gy"), 0, 0, tiled=True).reshape(T, C)
    (rows,) = call(
        sum_kernel,
        [block_zero(m) for m in reduce_rows(keep0, send0) + sums1 + sums2],
        [((T, MAIN), BF)],
    )
    rows = lax.all_to_all(rows.reshape(32, 8, MAIN), ("gz", "gx"), 0, 0, tiled=True)
    (grad,) = call(home_kernel, [grad, to_home], [tokens])
    (weight_grads,) = call(last_sum_kernel, [rows], [((6, 3 * C), F32)], vmem=16 << 20)
    return grad.reshape(cotangent.shape), weight_grads


def solution(mesh):
    in_specs = (
        P("gz", "gy", "gx", None),
        P(None, "gz", "gy", "gx", None),
        P(None, "gz", "gy", "gx", None),
        P(),
        P(),
        P(),
    )
    out_specs = (P("gz", "gy", "gx", None), P(("gz", "gy", "gx"), None))
    return jax.shard_map(
        per_device, mesh=mesh, in_specs=in_specs, out_specs=out_specs, check_vma=False
    )
```
